32 devices in a mesh: grp: 16 (over z, y, x), head: 2 (over core).
Axes of the slice: x: 2, y: 2, z: 4, core: 2. Of those that a mesh axis runs over, the one named last changes fastest.
Arguments:
- residual: bfloat16 [256, 2880], P('grp'), may hold values from -4 to 4
- queries: bfloat16 [256, 8, 256], P('grp', 'head'), may hold values from -200 to 200
- kv_cache: bfloat16 [256, 8, 128, 128], P('grp', 'head'), may hold values from -5 to 5
- new_kv: bfloat16 [256, 8, 128], P('grp', 'head'), may hold values from -5 to 5
- positions: int32 [256], P('grp'), may hold values from 0 to 383
- sink_logits: float32 [8, 4], P('head'), may hold values from 0 to 5
- out_proj: bfloat16 [8, 256, 2880], P('head'), may hold values from -0.375 to 0.375
- norm_gain: float32 [2880], replicated, may hold values from 0.5 to 1.5
- route_ids: int32 [256, 4], P('grp'), may hold values from 0 to 15, all different within a row; in each aligned block of 16 rows (0 to 15, 16 to 31, ...) at most 4 rows name the same one
- route_weights: int32 [256, 4], P('grp'), may hold values from 1 to 65535
- w_gate_up: bfloat16 [16, 2880, 2880], P('grp', None, 'head'), may hold values from -0.109375 to 0.109375
- w_down: bfloat16 [16, 1440, 2880], P('grp', 'head'), may hold values from -0.15625 to 0.15625
Outputs:
- layer_out: bfloat16 [256, 2880], P('grp', 'head')
The draws below stay inside these ranges and needn't reach their ends.
Inputs may be any that keep to these rules, and one draw needn't show every extreme that they name: `route_ids`: in the 16 rows of one index of grp, at most 4 rows name the same expert; each row names 4 different experts.
All inputs are finite; a program needn't handle non-finite values.
Results may differ from the reference program's by a relative error of at most 0.025.
Values may be sent and summed in bfloat16 or wider, within the bound.
A program may use at most 64 MiB of HBM per device.

```python
import math
import jax
import jax.numpy as jnp
import numpy as np
from jax import lax

D = 2880
HD = 64
KVH = 8
GQ = 4
WIN = 128
FFE = 1440
TOPK = 4
REQ_DEV = 16
CAP = 4
TOKENS = 256
EXPERTS = 16
N_GRP = 16


def attention_inputs(key):
    key_pos = jax.random.fold_in(key, 11)
    key_cycle = jax.random.fold_in(key, 12)
    key_query = jax.random.fold_in(key, 13)
    positions = jax.random.randint(key_pos, (TOKENS,), 0, 3 * WIN).astype(jnp.int32)
    positions = positions.at[0].set(3 * WIN - 1).at[1].set(0)
    cycle_cache = jax.random.truncated_normal(key_cycle, -5.0, 5.0, (TOKENS, KVH, WIN, 2 * HD), jnp.float32)
    queries = jax.random.truncated_normal(key_query, -5.0, 5.0, (TOKENS, KVH, GQ * HD), jnp.float32)
    return (positions, cycle_cache, queries)


def draw_positions(key, part):
    return attention_inputs(key)[0]


def draw_kv_cache(key, part):
    return attention_inputs(key)[1].astype(jnp.bfloat16)


def draw_queries(key, part):
    return attention_inputs(key)[2].astype(jnp.bfloat16)


def place_ends(entries, rng, low, top_value):
    extent = entries.shape
    index_at = [jax.random.randint(jax.random.fold_in(rng, axis), (), 0, extent[axis]) for axis in range(len(extent))]
    entries = entries.at[tuple(index_at)].set(low)
    longest = extent.index(max(extent))
    index_at[longest] = (index_at[longest] + 1) % extent[longest]
    return entries.at[tuple(index_at)].set(top_value)


def levels(key, dims, pieces, low, high):
    level, own = 1.0, jax.random.fold_in(key, 6)
    for axis_at, shards_of in pieces:
        draws = jnp.exp(jax.random.uniform(jax.random.fold_in(own, axis_at), (shards_of,), jnp.float32, low / len(pieces), high / len(pieces)))
        level = level * jnp.repeat(draws, dims[axis_at] // shards_of).reshape([-1 if axis == axis_at else 1 for axis in range(len(dims))])
    return level


def deal_out(key, own, number, rows, number_of, top, most, skew):
    ranking = jax.random.permutation(key, number_of)
    crowded, ordinary = load_shares(number_of, rows * top, most, skew, True), load_shares(number_of, rows * top, most, skew, False)
    places = jnp.arange(number_of)

    def named(tallies, offset_by):
        used = int((tallies > 0).sum())
        fixed = max(1, used // 4)
        passed = fixed + (places - fixed + offset_by * (used - fixed)) % max(1, number_of - fixed)
        return jnp.zeros((number_of,), jnp.int32).at[ranking[jnp.where(places < fixed, places, passed)]].set(jnp.asarray(tallies, jnp.int32))

    tallies = jnp.where(number % 4 == 0, named(crowded, number // 4), named(ordinary, number - number // 4 - 1))
    mixed = jax.random.permutation(jax.random.fold_in(own, 3), number_of)
    giver, taker = mixed[0:number_of // 2 * 2:2], mixed[1:number_of // 2 * 2:2]
    room = jnp.minimum(tallies[giver] - 1, most - tallies[taker]) // 2
    room = jnp.where((giver == ranking[0]) | (taker == ranking[0]) | (tallies[taker] == 0), 0, jnp.maximum(room, 0))
    passed = jax.random.randint(jax.random.fold_in(own, 4), (number_of // 2,), 0, 1 << 20) % (room + 1)
    tallies = tallies.at[giver].add(-passed).at[taker].add(passed)
    items = jnp.searchsorted(jnp.cumsum(tallies), jnp.arange(rows * top), side="right").astype(jnp.int32)
    table = items.reshape(top, rows).T
    table = table[jax.random.permutation(jax.random.fold_in(own, 1), rows)]
    offset_by = jax.random.randint(jax.random.fold_in(own, 2), (rows, 1), 0, top)
    return jnp.take_along_axis(table, (jnp.arange(top)[None, :] + offset_by) % top, axis=1)


def load_shares(amount, total, most, slope, full):
    loads = [(1 << 20) // math.isqrt(standing ** slope) + 1 for standing in range(1, amount + 1)]
    largest = most if full else min(most, max(-(-total // amount), total * loads[0] // sum(loads)))
    least = 1 if total - largest >= amount - 1 else 0
    given, surplus = [largest] + [least] * (amount - 1), total - largest - least * (amount - 1)
    while surplus > 0:
        candidates = [i for i in range(1, amount) if given[i] < largest] or [i for i in range(1, amount) if given[i] < most]
        mass, budget = sum([loads[i] for i in candidates]), surplus
        for i in candidates:
            more = min(most - given[i], max(1, budget * loads[i] // mass), surplus)
            given[i] = given[i] + more
            surplus = surplus - more
    return np.array(given)


def noise(key, shape, deviation, reach, pieces=(), kind=jnp.bfloat16):
    level = levels(key, shape, pieces, -0.22, 0.18) if pieces else 1.0
    array = jax.random.normal(key, shape, jnp.float32) * deviation * level
    return jnp.minimum(jnp.maximum(array, -reach), reach).astype(kind)


def setup_inputs(seed: int = 0) -> dict:
    streams_of = jax.random.split(jax.random.key(seed), 13)
    residual = noise(streams_of[0], (TOKENS, D), 0.5, 4.0, ((0, 16),))
    queries = draw_queries(jax.random.fold_in(streams_of[12], 71), 0)
    kv_cache = draw_kv_cache(jax.random.fold_in(streams_of[12], 71), 0)
    new_kv = noise(streams_of[3], (TOKENS, KVH, 2 * HD), 1.0, 5.0, ((0, 16), (1, 2)))
    positions = draw_positions(jax.random.fold_in(streams_of[12], 71), 0)
    sink_logits = jnp.clip(5.0 * jax.random.uniform(streams_of[5], (KVH, GQ), jnp.float32) ** levels(streams_of[5], (KVH, GQ), ((0, 2),), -0.2, 0.2), 0.0, 5.0)
    out_proj = noise(streams_of[6], (KVH, GQ * HD, D), (GQ * HD) ** -0.5, 0.375, ((0, 2),))
    norm_gain = jnp.clip(1.0 + 0.1 * jax.random.normal(streams_of[7], (D,), jnp.float32), 0.5, 1.5)
    route_ids_keys = jax.random.split(jax.random.fold_in(streams_of[8], 1), TOKENS // REQ_DEV)
    route_ids_turns = jax.random.permutation(jax.random.fold_in(streams_of[8], 3), TOKENS // REQ_DEV)
    route_ids = jax.vmap(lambda own, number: deal_out(jax.random.fold_in(streams_of[8], 2), own, number, REQ_DEV, EXPERTS, TOPK, CAP, 2))(route_ids_keys, route_ids_turns).reshape((TOKENS, TOPK))
    route_weights = place_ends(jax.random.randint(streams_of[9], (TOKENS, TOPK), 1, 65536), jax.random.fold_in(streams_of[9], 1), 1, 65535).astype(jnp.int32)
    w_gate_up = noise(streams_of[10], (EXPERTS, D, 2 * FFE), D ** -0.5, 0.109375, ((0, 16), (2, 2)))
    w_down = noise(streams_of[11], (EXPERTS, FFE, D), FFE ** -0.5, 0.15625, ((0, 16), (1, 2)))
    return {"residual": residual, "queries": queries, "kv_cache": kv_cache, "new_kv": new_kv, "positions": positions, "sink_logits": sink_logits, "out_proj": out_proj, "norm_gain": norm_gain, "route_ids": route_ids, "route_weights": route_weights, "w_gate_up": w_gate_up, "w_down": w_down}


epsilon = 1e-05
swish_alpha = 1.702

def rms_norm(values, gain):
    as_float = values.astype(jnp.float32)
    mean_square = lax.optimization_barrier(jnp.mean(as_float * as_float, axis=-1, keepdims=True))
    return (as_float * lax.rsqrt(mean_square + epsilon) * gain).astype(jnp.bfloat16)

def expert_apply(inputs):
    buffer_rows, gate_up, down_weight = inputs
    projected = jnp.dot(buffer_rows, gate_up, preferred_element_type=jnp.float32)
    pairs_view = projected.reshape(projected.shape[0], -1, 2)
    gate_half = pairs_view[..., 0]
    up_half = pairs_view[..., 1]
    activated = ((up_half + 1.0) * gate_half * jax.nn.sigmoid(swish_alpha * gate_half)).astype(jnp.bfloat16)
    return jnp.dot(activated, down_weight, preferred_element_type=jnp.float32)

def reference(residual, queries, kv_cache, new_kv, positions, sink_logits, out_proj, norm_gain, route_ids, route_weights, w_gate_up, w_down):
    slot_iota = jnp.arange(WIN, dtype=jnp.int32)
    current = positions % WIN
    slot_lag = (positions[:, None] - slot_iota[None, :]) % WIN
    is_valid = slot_lag <= positions[:, None]
    is_new = slot_iota[None, :] == current[:, None]
    merged = jnp.where(is_new[:, None, :, None], new_kv[:, :, None, :], kv_cache)
    key_part = merged[..., :HD].astype(jnp.float32)
    value_part = merged[..., HD:].astype(jnp.float32)
    query_part = queries.reshape(TOKENS, KVH, GQ, HD).astype(jnp.float32)
    scores = jnp.einsum('thgd,thwd->thgw', query_part, key_part) * HD ** (-0.5)
    scores = jnp.where(is_valid[:, None, None, :], scores, -jnp.inf)
    sink_col = sink_logits[None, :, :, None]
    largest = jnp.maximum(lax.optimization_barrier(jnp.max(scores, axis=-1, keepdims=True)), sink_col)
    weights_exp = jnp.exp(scores - largest)
    denominator = lax.optimization_barrier(jnp.sum(weights_exp, axis=-1, keepdims=True)) + jnp.exp(sink_col - largest)
    weights = (weights_exp / denominator).astype(jnp.bfloat16)
    mixed = jnp.einsum('thgw,thwd->thgd', weights.astype(jnp.float32), value_part).astype(jnp.bfloat16)
    attention = jnp.dot(mixed.reshape(TOKENS, KVH * GQ * HD), out_proj.reshape(KVH * GQ * HD, D), preferred_element_type=jnp.float32)
    hidden = (residual.astype(jnp.float32) + attention).astype(jnp.bfloat16)
    normed = rms_norm(hidden, norm_gain)
    per_block = REQ_DEV * TOPK
    grouped_ids = route_ids.reshape(N_GRP, per_block).astype(jnp.int32)
    assign_iota = jnp.arange(per_block, dtype=jnp.int32)
    earlier = (grouped_ids[:, :, None] == grouped_ids[:, None, :]) & (assign_iota[:, None] > assign_iota[None, :])
    slot_rank = lax.optimization_barrier(jnp.sum(earlier.astype(jnp.int32), axis=-1)).astype(jnp.int32)
    block_iota = jnp.arange(N_GRP, dtype=jnp.int32)[:, None]
    slot_index = (grouped_ids * (N_GRP * CAP) + block_iota * CAP + slot_rank).reshape(-1).astype(jnp.int32)
    total_slots = EXPERTS * N_GRP * CAP
    source_row = jnp.zeros((total_slots,), jnp.int32).at[slot_index].set((jnp.arange(TOKENS * TOPK, dtype=jnp.int32) // TOPK).astype(jnp.int32))
    filled = jnp.zeros((total_slots,), jnp.bool_).at[slot_index].set(True)
    buffers = jnp.where(filled[:, None], normed[source_row], jnp.zeros((), jnp.bfloat16)).reshape(EXPERTS, N_GRP * CAP, D)
    expert_outs = lax.map(expert_apply, (buffers, w_gate_up, w_down))
    picked = expert_outs.reshape(total_slots, D)[slot_index]
    weight_vec = route_weights.reshape(-1).astype(jnp.float32) / 65536.0
    mixture = lax.optimization_barrier(jnp.sum((picked * weight_vec[:, None]).reshape(TOKENS, TOPK, D), axis=1))
    return (hidden.astype(jnp.float32) + mixture).astype(jnp.bfloat16)
```

```python
import functools

import jax
import jax.numpy as jnp
from jax import lax
from jax.experimental import pallas as pl
from jax.experimental.pallas import tpu as pltpu
from jax.sharding import PartitionSpec as P

epsilon = 1e-05
swish_alpha = 1.702


def rms_norm(values, gain):
    as_float = values.astype(jnp.float32)
    mean_square = jnp.mean(as_float * as_float, axis=-1, keepdims=True)
    return (as_float * lax.rsqrt(mean_square + epsilon) * gain).astype(jnp.bfloat16)


def attend(queries, kv_cache, new_kv, positions, sink_logits):
    head_dim = new_kv.shape[2] // 2
    window = kv_cache.shape[2]
    row_count = queries.shape[0]
    kv_heads = queries.shape[1]
    groups = queries.shape[2] // head_dim
    slot_iota = jnp.arange(window, dtype=jnp.int32)
    current = positions % window
    slot_lag = (positions[:, None] - slot_iota[None, :]) % window
    is_valid = slot_lag <= positions[:, None]
    is_new = slot_iota[None, :] == current[:, None]
    merged = jnp.where(is_new[:, None, :, None], new_kv[:, :, None, :], kv_cache)
    key_part = merged[..., :head_dim]
    value_part = merged[..., head_dim:]
    query_part = queries.reshape(row_count, kv_heads, groups, head_dim)
    scores = jnp.einsum(
        "thgd,thwd->thgw", query_part, key_part, preferred_element_type=jnp.float32
    ) * head_dim ** (-0.5)
    scores = jnp.where(is_valid[:, None, None, :], scores, -jnp.inf)
    sink_col = sink_logits[None, :, :, None]
    largest = jnp.maximum(jnp.max(scores, axis=-1, keepdims=True), sink_col)
    weights_exp = jnp.exp(scores - largest)
    denominator = jnp.sum(weights_exp, axis=-1, keepdims=True) + jnp.exp(sink_col - largest)
    weights = (weights_exp / denominator).astype(jnp.bfloat16)
    mixed = jnp.einsum(
        "thgw,thwd->thgd", weights, value_part, preferred_element_type=jnp.float32
    ).astype(jnp.bfloat16)
    return mixed.reshape(row_count, kv_heads * groups * head_dim)


def local(
    residual,
    queries,
    kv_cache,
    new_kv,
    positions,
    sink_logits,
    out_proj,
    norm_gain,
    route_ids,
    route_weights,
    w_gate_up,
    w_down,
):
    row_count = residual.shape[0]
    width_all = out_proj.shape[2]
    share_width = width_all // lax.axis_size("head")
    share_start = lax.axis_index("head") * share_width
    mixed = attend(queries, kv_cache, new_kv, positions, sink_logits)
    partial_value = jnp.dot(
        mixed, out_proj.reshape(-1, width_all), preferred_element_type=jnp.float32
    )
    attention = lax.psum(partial_value.astype(jnp.bfloat16), "head").astype(jnp.float32)
    hidden_full = (residual.astype(jnp.float32) + attention).astype(jnp.bfloat16)
    sent_rows = rms_norm(hidden_full, norm_gain)
    hidden_here = lax.dynamic_slice_in_dim(hidden_full, share_start, share_width, 1)
    expert_count = lax.axis_size("grp")
    topk_count = route_ids.shape[1]
    capacity = max(2, row_count * topk_count // expert_count)
    flat_ids = route_ids.reshape(-1)
    assign_iota = jnp.arange(flat_ids.shape[0], dtype=jnp.int32)
    earlier = (flat_ids[:, None] == flat_ids[None, :]) & (
        assign_iota[:, None] > assign_iota[None, :]
    )
    slot_rank = jnp.sum(earlier.astype(jnp.int32), axis=1)
    slot_dest = flat_ids * capacity + slot_rank
    slot_iota = jnp.arange(expert_count * capacity, dtype=jnp.int32)
    send_table = (slot_iota[:, None] == slot_dest[None, :]).astype(jnp.bfloat16)
    take_table = (slot_dest[:, None] == slot_iota[None, :]).astype(jnp.float32)
    repeated = jnp.repeat(sent_rows, topk_count, axis=0)
    outgoing = jnp.dot(send_table, repeated, preferred_element_type=jnp.float32).astype(
        jnp.bfloat16
    )
    outgoing = outgoing.reshape(expert_count, capacity, -1)
    received = lax.all_to_all(outgoing, "grp", split_axis=0, concat_axis=0, tiled=True)
    item_lead = received.shape[0]
    item_count = received.shape[1]
    flat_rows = received.reshape(item_lead * item_count, -1)
    projected = jnp.dot(flat_rows, w_gate_up[0], preferred_element_type=jnp.float32)
    pairs_view = projected.reshape(item_lead * item_count, -1, 2)
    gate_half = pairs_view[..., 0]
    up_half = pairs_view[..., 1]
    activated = ((up_half + 1.0) * gate_half * jax.nn.sigmoid(swish_alpha * gate_half)).astype(
        jnp.bfloat16
    )
    down_part = jnp.dot(activated, w_down[0], preferred_element_type=jnp.float32).reshape(
        item_lead, item_count, -1
    )
    back_rows = lax.all_to_all(
        down_part.astype(jnp.bfloat16), "grp", split_axis=0, concat_axis=0, tiled=True
    ).astype(down_part.dtype)
    gathered = jnp.dot(
        take_table, back_rows.reshape(expert_count * capacity, -1), precision=lax.Precision.HIGHEST
    )
    weight_vec = route_weights.reshape(-1).astype(jnp.float32) / 65536.0
    mixture = jnp.sum((gathered * weight_vec[:, None]).reshape(row_count, topk_count, -1), axis=1)
    mixture = lax.psum_scatter(
        mixture.astype(jnp.bfloat16), "head", scatter_dimension=1, tiled=True
    ).astype(jnp.float32)
    return (hidden_here.astype(jnp.float32) + mixture).astype(jnp.bfloat16)


MESH = pl.DeviceIdType.MESH
NT = (((1,), (1,)), ((), ()))


def fused_fits(mesh, args):
    queries, kv_cache = args[1], args[2]
    grp, head = mesh.shape["grp"], mesh.shape["head"]
    rows, heads, width = queries.shape
    half = kv_cache.shape[3] // 2
    return (
        head == 2
        and grp % 4 == 0
        and kv_cache.shape[3] == 128
        and kv_cache.shape[2] % 128 == 0
        and (width // half) % 2 == 0
        and rows % 16 == 0
        and heads * (width // half) % 16 == 0
        and capacity_of(rows, args[8].shape[1], grp) == 4
    )


def capacity_of(rows, topk, experts):
    return max(2, rows * topk // experts)


def largest_part(count, limit):
    return max(size for size in range(16, limit + 1, 16) if count % size == 0)


def fused_kernel(
    n,
    residual,
    queries,
    new_kv,
    positions,
    sinks,
    gain,
    ids,
    route_w,
    kv_hbm,
    wo_hbm,
    wgu_hbm,
    wd_hbm,
    out,
    kv,
    wo,
    wgu,
    wd,
    q2,
    nv,
    mix,
    part_tx,
    part_rx,
    tx,
    rx,
    flat,
    x_in,
    proj,
    act,
    ex_tx,
    ex_rx,
    back_tx,
    back_rx,
    back_flat,
    local_sem,
    part_sem,
    disp_send,
    disp_recv,
    fwd_send,
    ex_send,
    ex_recv,
    back_send,
    back_recv,
):
    rows, width = residual.shape
    half = out.shape[1]
    heads = queries.shape[1]
    win, kv_width = kv.shape[2], kv.shape[3]
    hd = kv_width // 2
    groups = queries.shape[2] // hd
    qrows = heads * groups
    topk = ids.shape[0]
    cap = tx.shape[1]
    slots = n * cap
    hidden_units = wd.shape[0]
    f32, bf16 = jnp.float32, jnp.bfloat16

    b = lax.axis_index("grp")
    h = lax.axis_index("head")
    partner = 1 - h

    loads = [
        pltpu.make_async_copy(src, dst, local_sem.at[i])
        for i, (src, dst) in enumerate(
            ((kv_hbm, kv), (wo_hbm, wo), (wgu_hbm, wgu), (wd_hbm, wd))
        )
    ]
    for load in loads:
        load.start()

    barrier = pltpu.get_barrier_semaphore()
    pl.semaphore_signal(barrier, inc=1, device_id=(b, partner), device_id_type=MESH)

    def greet(d, carry):
        pl.semaphore_signal(
            barrier, inc=1, device_id=(lax.rem(b + d, n), h), device_id_type=MESH
        )
        return carry

    lax.fori_loop(1, n, greet, 0)

    lane = lax.broadcasted_iota(jnp.int32, (rows, heads, kv_width), 2)
    fresh = new_kv[...].astype(f32)
    for g in range(groups):
        at = g // 2 * kv_width
        piece = queries[:, :, at : at + kv_width].astype(f32)
        if g % 2:
            piece = pltpu.roll(piece, hd, 2)
        q2[:, g * heads : (g + 1) * heads, :] = jnp.where(lane < hd, piece, 0.0)
        nv[:, g * heads : (g + 1) * heads, :] = fresh

    row_iota = lax.broadcasted_iota(jnp.int32, (qrows, 1), 0)
    sink = jnp.zeros((qrows, 1), f32)
    for g in range(groups):
        for k in range(heads):
            sink = jnp.where(row_iota == g * heads + k, sinks[k, g], sink)
    r_iota = lax.broadcasted_iota(jnp.int32, (qrows, heads * win), 0)
    c_iota = lax.broadcasted_iota(jnp.int32, (qrows, heads * win), 1)
    own_block = lax.rem(r_iota, heads) == c_iota // win
    slot = lax.rem(c_iota, win)
    scale = hd ** (-0.5)

    loads[0].wait()

    def attend_one(t, carry):
        p = positions[t]
        cur = lax.rem(p, win)
        q = q2[t]
        new = nv[t]
        cache = kv[t].reshape(heads * win, kv_width)
        s = lax.dot_general(q.astype(bf16), cache, NT, preferred_element_type=f32) * scale
        s_new = jnp.sum(q * new, axis=1, keepdims=True) * scale
        is_new = slot == cur
        s = jnp.where(is_new, s_new, s)
        lag = cur - slot
        lag = jnp.where(lag < 0, lag + win, lag)
        s = jnp.where(own_block & (lag <= p), s, -jnp.inf)
        m = jnp.maximum(jnp.max(s, axis=1, keepdims=True), sink)
        e = jnp.exp(s - m)
        inv = 1.0 / (jnp.sum(e, axis=1, keepdims=True) + jnp.exp(sink - m))
        w = e * inv
        w_old = jnp.where(is_new, 0.0, w).astype(bf16)
        w_new = jnp.sum(jnp.where(is_new, w, 0.0), axis=1, keepdims=True).astype(bf16).astype(f32)
        o = jnp.dot(w_old, cache, preferred_element_type=f32) + w_new * new
        mix[pl.ds(pl.multiple_of(t * qrows, qrows), qrows), :] = o
        return carry

    lax.fori_loop(0, rows, attend_one, 0, unroll=4)

    lane2 = lax.broadcasted_iota(jnp.int32, (rows, kv_width), 1)
    loads[1].wait()
    acc = jnp.zeros((rows, width), f32)
    for k in range(heads):
        pairs = []
        for g in range(0, groups, 2):
            even = mix[pl.ds(g * heads + k, rows, stride=qrows), :]
            odd = mix[pl.ds((g + 1) * heads + k, rows, stride=qrows), :]
            pairs.append(jnp.where(lane2 < hd, pltpu.roll(even, hd, 1), odd))
        mixed = jnp.concatenate(pairs, axis=1).astype(bf16)
        acc += lax.dot_general(mixed, wo[k], NT, preferred_element_type=f32)
    part_tx[...] = acc.astype(bf16)

    pl.semaphore_wait(barrier, n)
    part = pltpu.make_async_remote_copy(
        src_ref=part_tx,
        dst_ref=part_rx,
        send_sem=part_sem.at[0],
        recv_sem=part_sem.at[1],
        device_id=(b, partner),
        device_id_type=MESH,
    )
    part.start()

    t_row = lax.broadcasted_iota(jnp.int32, (slots, rows), 0)
    rel, slot_c = t_row // cap, lax.rem(t_row, cap)
    named = jnp.zeros((slots, rows), jnp.int32)
    weight = jnp.zeros((slots, rows), jnp.int32)
    for k in range(topk):
        other = ids[k : k + 1, :] - b
        other = jnp.where(other < 0, other + n, other)
        hit = rel == other
        named = jnp.where(hit, 1, named)
        weight = jnp.where(hit, route_w[k : k + 1, :], weight)
    before = (
        lax.broadcasted_iota(jnp.int32, (rows, rows), 0)
        < lax.broadcasted_iota(jnp.int32, (rows, rows), 1)
    )
    rank = jnp.dot(
        named.astype(f32).astype(bf16),
        before.astype(f32).astype(bf16),
        preferred_element_type=f32,
    )
    chosen = (named > 0) & (rank == slot_c.astype(f32))
    table = chosen.astype(f32).astype(bf16)
    weight = jnp.where(chosen, weight, 0)
    high = weight // 256
    low = weight - high * 256
    eye = (
        lax.broadcasted_iota(jnp.int32, (rows, rows), 0)
        == lax.broadcasted_iota(jnp.int32, (rows, rows), 1)
    )
    eye = eye.astype(f32).astype(bf16)
    comb_high = lax.dot_general(
        eye, high.astype(f32).astype(bf16), NT, preferred_element_type=f32
    ).astype(bf16)
    comb_low = lax.dot_general(
        eye, low.astype(f32).astype(bf16), NT, preferred_element_type=f32
    ).astype(bf16)

    part.wait()
    attention = part_tx[...].astype(f32) + part_rx[...].astype(f32)
    hidden = (residual[...].astype(f32) + attention).astype(bf16).astype(f32)
    mean_square = jnp.sum(hidden * hidden, axis=1, keepdims=True) * (1.0 / width)
    normed = (hidden * lax.rsqrt(mean_square + epsilon) * gain[...]).astype(bf16)
    outgoing = jnp.dot(table, normed, preferred_element_type=f32)
    flat[0:cap, :] = outgoing[0:cap]
    for d in range(1, n):
        tx[d] = outgoing[d * cap : (d + 1) * cap].astype(bf16)

    def disp(d):
        return pltpu.make_async_remote_copy(
            src_ref=tx.at[d],
            dst_ref=rx.at[d],
            send_sem=disp_send.at[d],
            recv_sem=disp_recv.at[d],
            device_id=(lax.rem(b + d, n), h),
            device_id_type=MESH,
        )

    def fwd(d):
        return pltpu.make_async_remote_copy(
            src_ref=rx.at[d],
            dst_ref=rx.at[d],
            send_sem=fwd_send.at[d],
            recv_sem=disp_recv.at[d],
            device_id=(b, partner),
            device_id_type=MESH,
        )

    def each(offset, action):
        def step(j, carry):
            d = 2 * j + offset

            @pl.when(d > 0)
            def _():
                action(d)

            return carry

        lax.fori_loop(0, n // 2, step, 0)

    def pass_on(d):
        disp(d).wait_recv()
        fwd(d).start()

    each(h, lambda d: disp(d).start())
    each(h, pass_on)
    each(partner, lambda d: fwd(d).wait_recv())

    for d in range(1, n):
        flat[d * cap : (d + 1) * cap, :] = rx[d].astype(f32)
    x_in[...] = flat[...].astype(bf16)

    loads[2].wait()
    step_rows = largest_part(wgu.shape[0], 256)

    def gate_up(i, carry):
        at = pl.ds(pl.multiple_of(i * step_rows, step_rows), step_rows)
        proj[at, 0:slots] = lax.dot_general(
            wgu[at, :], x_in[...], NT, preferred_element_type=f32
        )
        return carry

    lax.fori_loop(0, wgu.shape[0] // step_rows, gate_up, 0)

    gate = proj[pl.ds(0, hidden_units, stride=2), :]
    up = proj[pl.ds(1, hidden_units, stride=2), :]
    act[0:hidden_units, :] = (up + 1.0) * gate * (1.0 / (1.0 + jnp.exp(-swish_alpha * gate)))
    if act.shape[0] > hidden_units:
        act[hidden_units:, :] = jnp.zeros((act.shape[0] - hidden_units, act.shape[1]), f32)
    activated = act[...].T[0:slots, 0:hidden_units].astype(bf16)

    loads[3].wait()
    down = jnp.dot(activated, wd[...], preferred_element_type=f32)
    left, right = down[:, 0:half], down[:, half:width]
    mine = jnp.where(h == 0, left, right)
    ex_tx[...] = jnp.where(h == 0, right, left).astype(bf16)

    def exchange(i):
        at = pl.ds(i * 16, 16)
        return pltpu.make_async_remote_copy(
            src_ref=ex_tx.at[at, :],
            dst_ref=ex_rx.at[at, :],
            send_sem=ex_send.at[i],
            recv_sem=ex_recv.at[i],
            device_id=(b, partner),
            device_id_type=MESH,
        )

    def give_back(d):
        return pltpu.make_async_remote_copy(
            src_ref=back_tx.at[d],
            dst_ref=back_rx.at[d],
            send_sem=back_send.at[d],
            recv_sem=back_recv.at[d],
            device_id=(lax.rem(b + n - d, n), h),
            device_id_type=MESH,
        )

    parts = slots // 16
    per_part = 16 // cap
    for i in range(parts):
        exchange(i).start()
    for i in range(parts):
        exchange(i).wait_recv()
        total = mine[i * 16 : (i + 1) * 16] + ex_rx[i * 16 : (i + 1) * 16, :].astype(f32)
        for j in range(per_part):
            d = i * per_part + j
            block = total[j * cap : (j + 1) * cap]
            if d == 0:
                back_flat[0:cap, :] = block
            else:
                back_tx[d] = block.astype(bf16)
                give_back(d).start()

    hidden_here = jnp.where(h == 0, hidden[:, 0:half], hidden[:, half:width])

    for d in range(1, n):
        give_back(d).wait_recv()
        back_flat[d * cap : (d + 1) * cap, :] = back_rx[d].astype(f32)
    rows_back = back_flat[...].astype(bf16)
    mixture = jnp.dot(comb_high, rows_back, preferred_element_type=f32) * (1.0 / 256)
    mixture += jnp.dot(comb_low, rows_back, preferred_element_type=f32) * (1.0 / 65536)
    out[...] = (hidden_here + mixture).astype(bf16)

    each(h, lambda d: disp(d).wait_send())
    each(h, lambda d: fwd(d).wait_send())
    for i in range(parts):
        exchange(i).wait_send()

    def sent(d, carry):
        give_back(d).wait_send()
        return carry

    lax.fori_loop(1, n, sent, 0)


def fused(
    n,
    residual,
    queries,
    kv_cache,
    new_kv,
    positions,
    sink_logits,
    out_proj,
    norm_gain,
    route_ids,
    route_weights,
    w_gate_up,
    w_down,
):
    rows, width = residual.shape
    half = width // 2
    heads = queries.shape[1]
    kv_width = kv_cache.shape[3]
    groups = queries.shape[2] * 2 // kv_width
    cap = capacity_of(rows, route_ids.shape[1], n)
    slots = n * cap
    lanes = -(-slots // 128) * 128
    units = w_down.shape[1]
    f32, bf16 = jnp.float32, jnp.bfloat16
    vmem = pl.BlockSpec(memory_space=pltpu.VMEM)
    smem = pl.BlockSpec(memory_space=pltpu.SMEM)
    hbm = pl.BlockSpec(memory_space=pl.ANY)
    dma = pltpu.SemaphoreType.DMA
    wo = jnp.swapaxes(out_proj, 1, 2)
    wgu = jnp.swapaxes(w_gate_up[0], 0, 1)
    wd = w_down[0]
    return pl.pallas_call(
        functools.partial(fused_kernel, n),
        out_shape=jax.ShapeDtypeStruct((rows, half), bf16),
        in_specs=[vmem, vmem, vmem, smem, smem, vmem, vmem, vmem, hbm, hbm, hbm, hbm],
        out_specs=vmem,
        scratch_shapes=[
            pltpu.VMEM(kv_cache.shape, bf16),
            pltpu.VMEM(wo.shape, bf16),
            pltpu.VMEM(wgu.shape, bf16),
            pltpu.VMEM(wd.shape, bf16),
            pltpu.VMEM((rows, heads * groups, kv_width), f32),
            pltpu.VMEM((rows, heads * groups, kv_width), f32),
            pltpu.VMEM((rows * heads * groups, kv_width), f32),
            pltpu.VMEM((rows, width), bf16),
            pltpu.VMEM((rows, width), bf16),
            pltpu.VMEM((n, cap, width), bf16),
            pltpu.VMEM((n, cap, width), bf16),
            pltpu.VMEM((slots, width), f32),
            pltpu.VMEM((slots, width), bf16),
            pltpu.VMEM((2 * units, lanes), f32),
            pltpu.VMEM((-(-units // 128) * 128, lanes), f32),
            pltpu.VMEM((slots, half), bf16),
            pltpu.VMEM((slots, half), bf16),
            pltpu.VMEM((n, cap, half), bf16),
            pltpu.VMEM((n, cap, half), bf16),
            pltpu.VMEM((slots, half), f32),
            dma((4,)),
            dma((2,)),
            dma((n,)),
            dma((n,)),
            dma((n,)),
            dma((slots // 16,)),
            dma((slots // 16,)),
            dma((n,)),
            dma((n,)),
        ],
        compiler_params=pltpu.CompilerParams(
            collective_id=0, has_side_effects=True, vmem_limit_bytes=48 * 1024 * 1024
        ),
    )(
        residual,
        queries,
        new_kv,
        positions,
        sink_logits,
        norm_gain.reshape(1, width),
        route_ids.T,
        route_weights.T,
        kv_cache,
        wo,
        wgu,
        wd,
    )


def solution(mesh):
    in_specs = (
        P("grp", None),
        P("grp", "head", None),
        P("grp", "head", None, None),
        P("grp", "head", None),
        P("grp"),
        P("head", None),
        P("head", None, None),
        P(),
        P("grp", None),
        P("grp", None),
        P("grp", None, "head"),
        P("grp", "head", None),
    )
    out_specs = P("grp", "head")
    def body(*args):
        if fused_fits(mesh, args):
            return fused(mesh.shape["grp"], *args)
        return local(*args)

    return jax.shard_map(body, mesh=mesh, in_specs=in_specs, out_specs=out_specs, check_vma=False)
```

```python
import functools

import jax
import jax.numpy as jnp
from jax import lax
from jax.experimental import pallas as pl
from jax.experimental.pallas import tpu as pltpu
from jax.sharding import PartitionSpec as P

epsilon = 1e-05
swish_alpha = 1.702


def rms_norm(values, gain):
    as_float = values.astype(jnp.float32)
    mean_square = jnp.mean(as_float * as_float, axis=-1, keepdims=True)
    return (as_float * lax.rsqrt(mean_square + epsilon) * gain).astype(jnp.bfloat16)


def attend(queries, kv_cache, new_kv, positions, sink_logits):
    head_dim = new_kv.shape[2] // 2
    window = kv_cache.shape[2]
    row_count = queries.shape[0]
    kv_heads = queries.shape[1]
    groups = queries.shape[2] // head_dim
    slot_iota = jnp.arange(window, dtype=jnp.int32)
    current = positions % window
    slot_lag = (positions[:, None] - slot_iota[None, :]) % window
    is_valid = slot_lag <= positions[:, None]
    is_new = slot_iota[None, :] == current[:, None]
    merged = jnp.where(is_new[:, None, :, None], new_kv[:, :, None, :], kv_cache)
    key_part = merged[..., :head_dim]
    value_part = merged[..., head_dim:]
    query_part = queries.reshape(row_count, kv_heads, groups, head_dim)
    scores = jnp.einsum(
        "thgd,thwd->thgw", query_part, key_part, preferred_element_type=jnp.float32
    ) * head_dim ** (-0.5)
    scores = jnp.where(is_valid[:, None, None, :], scores, -jnp.inf)
    sink_col = sink_logits[None, :, :, None]
    largest = jnp.maximum(jnp.max(scores, axis=-1, keepdims=True), sink_col)
    weights_exp = jnp.exp(scores - largest)
    denominator = jnp.sum(weights_exp, axis=-1, keepdims=True) + jnp.exp(sink_col - largest)
    weights = (weights_exp / denominator).astype(jnp.bfloat16)
    mixed = jnp.einsum(
        "thgw,thwd->thgd", weights, value_part, preferred_element_type=jnp.float32
    ).astype(jnp.bfloat16)
    return mixed.reshape(row_count, kv_heads * groups * head_dim)


def local(
    residual,
    queries,
    kv_cache,
    new_kv,
    positions,
    sink_logits,
    out_proj,
    norm_gain,
    route_ids,
    route_weights,
    w_gate_up,
    w_down,
):
    row_count = residual.shape[0]
    width_all = out_proj.shape[2]
    share_width = width_all // lax.axis_size("head")
    share_start = lax.axis_index("head") * share_width
    mixed = attend(queries, kv_cache, new_kv, positions, sink_logits)
    partial_value = jnp.dot(
        mixed, out_proj.reshape(-1, width_all), preferred_element_type=jnp.float32
    )
    attention = lax.psum(partial_value.astype(jnp.bfloat16), "head").astype(jnp.float32)
    hidden_full = (residual.astype(jnp.float32) + attention).astype(jnp.bfloat16)
    sent_rows = rms_norm(hidden_full, norm_gain)
    hidden_here = lax.dynamic_slice_in_dim(hidden_full, share_start, share_width, 1)
    expert_count = lax.axis_size("grp")
    topk_count = route_ids.shape[1]
    capacity = max(2, row_count * topk_count // expert_count)
    flat_ids = route_ids.reshape(-1)
    assign_iota = jnp.arange(flat_ids.shape[0], dtype=jnp.int32)
    earlier = (flat_ids[:, None] == flat_ids[None, :]) & (
        assign_iota[:, None] > assign_iota[None, :]
    )
    slot_rank = jnp.sum(earlier.astype(jnp.int32), axis=1)
    slot_dest = flat_ids * capacity + slot_rank
    slot_iota = jnp.arange(expert_count * capacity, dtype=jnp.int32)
    send_table = (slot_iota[:, None] == slot_dest[None, :]).astype(jnp.bfloat16)
    take_table = (slot_dest[:, None] == slot_iota[None, :]).astype(jnp.float32)
    repeated = jnp.repeat(sent_rows, topk_count, axis=0)
    outgoing = jnp.dot(send_table, repeated, preferred_element_type=jnp.float32).astype(
        jnp.bfloat16
    )
    outgoing = outgoing.reshape(expert_count, capacity, -1)
    received = lax.all_to_all(outgoing, "grp", split_axis=0, concat_axis=0, tiled=True)
    item_lead = received.shape[0]
    item_count = received.shape[1]
    flat_rows = received.reshape(item_lead * item_count, -1)
    projected = jnp.dot(flat_rows, w_gate_up[0], preferred_element_type=jnp.float32)
    pairs_view = projected.reshape(item_lead * item_count, -1, 2)
    gate_half = pairs_view[..., 0]
    up_half = pairs_view[..., 1]
    activated = ((up_half + 1.0) * gate_half * jax.nn.sigmoid(swish_alpha * gate_half)).astype(
        jnp.bfloat16
    )
    down_part = jnp.dot(activated, w_down[0], preferred_element_type=jnp.float32).reshape(
        item_lead, item_count, -1
    )
    back_rows = lax.all_to_all(
        down_part.astype(jnp.bfloat16), "grp", split_axis=0, concat_axis=0, tiled=True
    ).astype(down_part.dtype)
    gathered = jnp.dot(
        take_table, back_rows.reshape(expert_count * capacity, -1), precision=lax.Precision.HIGHEST
    )
    weight_vec = route_weights.reshape(-1).astype(jnp.float32) / 65536.0
    mixture = jnp.sum((gathered * weight_vec[:, None]).reshape(row_count, topk_count, -1), axis=1)
    mixture = lax.psum_scatter(
        mixture.astype(jnp.bfloat16), "head", scatter_dimension=1, tiled=True
    ).astype(jnp.float32)
    return (hidden_here.astype(jnp.float32) + mixture).astype(jnp.bfloat16)


MESH = pl.DeviceIdType.MESH
NT = (((1,), (1,)), ((), ()))


def fused_fits(mesh, args):
    queries, kv_cache = args[1], args[2]
    grp, head = mesh.shape["grp"], mesh.shape["head"]
    rows, heads, width = queries.shape
    half = kv_cache.shape[3] // 2
    return (
        head == 2
        and grp % 4 == 0
        and kv_cache.shape[3] == 128
        and kv_cache.shape[2] % 128 == 0
        and (width // half) % 2 == 0
        and rows % 16 == 0
        and heads * (width // half) % 16 == 0
        and capacity_of(rows, args[8].shape[1], grp) == 4
    )


def capacity_of(rows, topk, experts):
    return max(2, rows * topk // experts)


def largest_part(count, limit):
    return max(size for size in range(16, limit + 1, 16) if count % size == 0)


def fused_kernel(
    n,
    positions_hbm,
    sinks_hbm,
    queries_hbm,
    new_kv_hbm,
    kv_hbm,
    wo_hbm,
    ids_hbm,
    route_w_hbm,
    residual_hbm,
    gain_hbm,
    wgu_hbm,
    wd_hbm,
    out,
    positions,
    sinks,
    queries,
    new_kv,
    ids,
    route_w,
    residual,
    gain,
    kv,
    wo,
    wgu,
    wd,
    q2,
    nv,
    mix,
    part_tx,
    part_rx,
    tx,
    rx,
    flat,
    x_in,
    proj,
    act,
    ex_tx,
    ex_rx,
    back_tx,
    back_rx,
    back_flat,
    local_sem,
    part_sem,
    disp_send,
    disp_recv,
    fwd_send,
    ex_send,
    ex_recv,
    back_send,
    back_recv,
):
    rows, width = residual.shape
    half = out.shape[1]
    heads = queries.shape[1]
    win, kv_width = kv.shape[2], kv.shape[3]
    hd = kv_width // 2
    groups = queries.shape[2] // hd
    qrows = heads * groups
    topk = ids.shape[0]
    cap = tx.shape[1]
    slots = n * cap
    hidden_units = wd.shape[0]
    f32, bf16 = jnp.float32, jnp.bfloat16

    b = lax.axis_index("grp")
    h = lax.axis_index("head")
    partner = 1 - h

    loads = [
        pltpu.make_async_copy(src, dst, local_sem.at[i])
        for i, (src, dst) in enumerate(
            (
                (positions_hbm, positions),
                (sinks_hbm, sinks),
                (queries_hbm, queries),
                (new_kv_hbm, new_kv),
                (kv_hbm, kv),
                (wo_hbm, wo),
                (ids_hbm, ids),
                (route_w_hbm, route_w),
                (residual_hbm, residual),
                (gain_hbm, gain),
                (wgu_hbm, wgu),
                (wd_hbm, wd),
            )
        )
    ]
    for load in loads[0:10]:
        load.start()

    barrier = pltpu.get_barrier_semaphore()
    pl.semaphore_signal(barrier, inc=1, device_id=(b, partner), device_id_type=MESH)

    def greet(d, carry):
        pl.semaphore_signal(
            barrier, inc=1, device_id=(lax.rem(b + d, n), h), device_id_type=MESH
        )
        return carry

    lax.fori_loop(1, n, greet, 0)

    for load in loads[0:4]:
        load.wait()

    lane = lax.broadcasted_iota(jnp.int32, (rows, heads, kv_width), 2)
    fresh = new_kv[...].astype(f32)
    for g in range(groups):
        at = g // 2 * kv_width
        piece = queries[:, :, at : at + kv_width].astype(f32)
        if g % 2:
            piece = pltpu.roll(piece, hd, 2)
        q2[:, g * heads : (g + 1) * heads, :] = jnp.where(lane < hd, piece, 0.0)
        nv[:, g * heads : (g + 1) * heads, :] = fresh

    row_iota = lax.broadcasted_iota(jnp.int32, (qrows, 1), 0)
    sink = jnp.zeros((qrows, 1), f32)
    for g in range(groups):
        for k in range(heads):
            sink = jnp.where(row_iota == g * heads + k, sinks[k, g], sink)
    r_iota = lax.broadcasted_iota(jnp.int32, (qrows, heads * win), 0)
    c_iota = lax.broadcasted_iota(jnp.int32, (qrows, heads * win), 1)
    own_block = lax.rem(r_iota, heads) == c_iota // win
    slot = lax.rem(c_iota, win)
    scale = hd ** (-0.5)

    loads[4].wait()

    def attend_one(t, carry):
        p = positions[t]
        cur = lax.rem(p, win)
        q = q2[t]
        new = nv[t]
        cache = kv[t].reshape(heads * win, kv_width)
        s = lax.dot_general(q.astype(bf16), cache, NT, preferred_element_type=f32) * scale
        s_new = jnp.sum(q * new, axis=1, keepdims=True) * scale
        is_new = slot == cur
        s = jnp.where(is_new, s_new, s)
        lag = cur - slot
        lag = jnp.where(lag < 0, lag + win, lag)
        s = jnp.where(own_block & (lag <= p), s, -jnp.inf)
        m = jnp.maximum(jnp.max(s, axis=1, keepdims=True), sink)
        e = jnp.exp(s - m)
        inv = 1.0 / (jnp.sum(e, axis=1, keepdims=True) + jnp.exp(sink - m))
        w = e * inv
        w_old = jnp.where(is_new, 0.0, w).astype(bf16)
        w_new = jnp.sum(jnp.where(is_new, w, 0.0), axis=1, keepdims=True).astype(bf16).astype(f32)
        o = jnp.dot(w_old, cache, preferred_element_type=f32) + w_new * new
        mix[pl.ds(pl.multiple_of(t * qrows, qrows), qrows), :] = o
        return carry

    lax.fori_loop(0, rows, attend_one, 0, unroll=8)

    lane2 = lax.broadcasted_iota(jnp.int32, (rows, kv_width), 1)
    loads[5].wait()
    for load in loads[10:]:
        load.start()
    acc = jnp.zeros((rows, width), f32)
    for k in range(heads):
        pairs = []
        for g in range(0, groups, 2):
            even = mix[pl.ds(g * heads + k, rows, stride=qrows), :]
            odd = mix[pl.ds((g + 1) * heads + k, rows, stride=qrows), :]
            pairs.append(jnp.where(lane2 < hd, pltpu.roll(even, hd, 1), odd))
        mixed = jnp.concatenate(pairs, axis=1).astype(bf16)
        acc += lax.dot_general(mixed, wo[k], NT, preferred_element_type=f32)
    part_tx[...] = acc.astype(bf16)

    pl.semaphore_wait(barrier, n)
    part = pltpu.make_async_remote_copy(
        src_ref=part_tx,
        dst_ref=part_rx,
        send_sem=part_sem.at[0],
        recv_sem=part_sem.at[1],
        device_id=(b, partner),
        device_id_type=MESH,
    )
    part.start()

    for load in loads[6:10]:
        load.wait()

    t_row = lax.broadcasted_iota(jnp.int32, (slots, rows), 0)
    rel, slot_c = t_row // cap, lax.rem(t_row, cap)
    named = jnp.zeros((slots, rows), jnp.int32)
    weight = jnp.zeros((slots, rows), jnp.int32)
    for k in range(topk):
        other = ids[k : k + 1, :] - b
        other = jnp.where(other < 0, other + n, other)
        hit = rel == other
        named = jnp.where(hit, 1, named)
        weight = jnp.where(hit, route_w[k : k + 1, :], weight)
    before = (
        lax.broadcasted_iota(jnp.int32, (rows, rows), 0)
        < lax.broadcasted_iota(jnp.int32, (rows, rows), 1)
    )
    rank = jnp.dot(
        named.astype(f32).astype(bf16),
        before.astype(f32).astype(bf16),
        preferred_element_type=f32,
    )
    chosen = (named > 0) & (rank == slot_c.astype(f32))
    table = chosen.astype(f32).astype(bf16)
    weight = jnp.where(chosen, weight, 0)
    high = weight // 256
    low = weight - high * 256
    eye = (
        lax.broadcasted_iota(jnp.int32, (rows, rows), 0)
        == lax.broadcasted_iota(jnp.int32, (rows, rows), 1)
    )
    eye = eye.astype(f32).astype(bf16)
    comb_high = lax.dot_general(
        eye, high.astype(f32).astype(bf16), NT, preferred_element_type=f32
    ).astype(bf16)
    comb_low = lax.dot_general(
        eye, low.astype(f32).astype(bf16), NT, preferred_element_type=f32
    ).astype(bf16)

    part.wait()
    attention = part_tx[...].astype(f32) + part_rx[...].astype(f32)
    hidden = (residual[...].astype(f32) + attention).astype(bf16).astype(f32)
    mean_square = jnp.sum(hidden * hidden, axis=1, keepdims=True) * (1.0 / width)
    normed = (hidden * lax.rsqrt(mean_square + epsilon) * gain[...].reshape(1, width)).astype(bf16)
    outgoing = jnp.dot(table, normed, preferred_element_type=f32)
    flat[0:cap, :] = outgoing[0:cap]
    for d in range(1, n):
        tx[d] = outgoing[d * cap : (d + 1) * cap].astype(bf16)

    def disp(d):
        return pltpu.make_async_remote_copy(
            src_ref=tx.at[d],
            dst_ref=rx.at[d],
            send_sem=disp_send.at[d],
            recv_sem=disp_recv.at[d],
            device_id=(lax.rem(b + d, n), h),
            device_id_type=MESH,
        )

    def fwd(d):
        return pltpu.make_async_remote_copy(
            src_ref=rx.at[d],
            dst_ref=rx.at[d],
            send_sem=fwd_send.at[d],
            recv_sem=disp_recv.at[d],
            device_id=(b, partner),
            device_id_type=MESH,
        )

    def each(parity, action, near_first=False):
        def step(j, carry):
            j = n // 2 - 1 - j if near_first else j
            even = (j + 1) // 2 * 2 * (1 - j % 2 * 2)
            odd = (j // 2 * 2 + 1) * (j % 2 * 2 - 1)
            d = n // 2 + parity * odd + (1 - parity) * even

            @pl.when(d > 0)
            def _():
                action(d)

            return carry

        lax.fori_loop(0, n // 2, step, 0)

    def pass_on(d):
        disp(d).wait_recv()
        fwd(d).start()

    each(h, lambda d: disp(d).start())
    each(h, pass_on, near_first=True)
    each(partner, lambda d: fwd(d).wait_recv(), near_first=True)

    for d in range(1, n):
        flat[d * cap : (d + 1) * cap, :] = rx[d].astype(f32)
    x_in[...] = flat[...].astype(bf16)

    loads[10].wait()
    step_rows = largest_part(wgu.shape[0], 480)

    def gate_up(i, carry):
        at = pl.ds(pl.multiple_of(i * step_rows, step_rows), step_rows)
        proj[at, 0:slots] = lax.dot_general(
            wgu[at, :], x_in[...], NT, preferred_element_type=f32
        )
        return carry

    lax.fori_loop(0, wgu.shape[0] // step_rows, gate_up, 0)

    gate = proj[pl.ds(0, hidden_units, stride=2), :]
    up = proj[pl.ds(1, hidden_units, stride=2), :]
    act[0:hidden_units, :] = (up + 1.0) * gate * (1.0 / (1.0 + jnp.exp(-swish_alpha * gate)))
    if act.shape[0] > hidden_units:
        act[hidden_units:, :] = jnp.zeros((act.shape[0] - hidden_units, act.shape[1]), f32)
    activated = act[...].T[0:slots, 0:hidden_units].astype(bf16)

    loads[11].wait()
    down = jnp.dot(activated, wd[...], preferred_element_type=f32)
    left, right = down[:, 0:half], down[:, half:width]
    mine = jnp.where(h == 0, left, right)
    ex_tx[...] = jnp.where(h == 0, right, left).astype(bf16)

    def exchange(i):
        at = pl.ds(i * 16, 16)
        return pltpu.make_async_remote_copy(
            src_ref=ex_tx.at[at, :],
            dst_ref=ex_rx.at[at, :],
            send_sem=ex_send.at[i],
            recv_sem=ex_recv.at[i],
            device_id=(b, partner),
            device_id_type=MESH,
        )

    def give_back(d):
        return pltpu.make_async_remote_copy(
            src_ref=back_tx.at[d],
            dst_ref=back_rx.at[d],
            send_sem=back_send.at[d],
            recv_sem=back_recv.at[d],
            device_id=(lax.rem(b + n - d, n), h),
            device_id_type=MESH,
        )

    parts = slots // 16
    per_part = 16 // cap
    far_first = sorted(range(parts), key=lambda i: abs(2 * i + 1 - parts))
    for i in far_first:
        exchange(i).start()
    for i in far_first:
        exchange(i).wait_recv()
        total = mine[i * 16 : (i + 1) * 16] + ex_rx[i * 16 : (i + 1) * 16, :].astype(f32)
        for j in range(per_part):
            d = i * per_part + j
            block = total[j * cap : (j + 1) * cap]
            if d == 0:
                back_flat[0:cap, :] = block
            else:
                back_tx[d] = block.astype(bf16)
                give_back(d).start()

    hidden_here = jnp.where(h == 0, hidden[:, 0:half], hidden[:, half:width])

    for d in range(1, n):
        give_back(d).wait_recv()
        back_flat[d * cap : (d + 1) * cap, :] = back_rx[d].astype(f32)
    rows_back = back_flat[...].astype(bf16)
    mixture = jnp.dot(comb_high, rows_back, preferred_element_type=f32) * (1.0 / 256)
    mixture += jnp.dot(comb_low, rows_back, preferred_element_type=f32) * (1.0 / 65536)
    out[...] = (hidden_here + mixture).astype(bf16)

    each(h, lambda d: disp(d).wait_send())
    each(h, lambda d: fwd(d).wait_send())
    for i in range(parts):
        exchange(i).wait_send()

    def sent(d, carry):
        give_back(d).wait_send()
        return carry

    lax.fori_loop(1, n, sent, 0)


def fused(
    n,
    residual,
    queries,
    kv_cache,
    new_kv,
    positions,
    sink_logits,
    out_proj,
    norm_gain,
    route_ids,
    route_weights,
    w_gate_up,
    w_down,
):
    rows, width = residual.shape
    half = width // 2
    heads = queries.shape[1]
    kv_width = kv_cache.shape[3]
    groups = queries.shape[2] * 2 // kv_width
    cap = capacity_of(rows, route_ids.shape[1], n)
    slots = n * cap
    lanes = -(-slots // 128) * 128
    units = w_down.shape[1]
    f32, bf16 = jnp.float32, jnp.bfloat16
    vmem = pl.BlockSpec(memory_space=pltpu.VMEM)
    hbm = pl.BlockSpec(memory_space=pl.ANY)
    dma = pltpu.SemaphoreType.DMA
    wo = jnp.swapaxes(out_proj, 1, 2)
    wgu = jnp.swapaxes(w_gate_up[0], 0, 1)
    wd = w_down[0]
    return pl.pallas_call(
        functools.partial(fused_kernel, n),
        out_shape=jax.ShapeDtypeStruct((rows, half), bf16),
        in_specs=[hbm] * 12,
        out_specs=vmem,
        scratch_shapes=[
            pltpu.SMEM(positions.shape, jnp.int32),
            pltpu.SMEM(sink_logits.shape, f32),
            pltpu.VMEM(queries.shape, bf16),
            pltpu.VMEM(new_kv.shape, bf16),
            pltpu.VMEM(route_ids.shape[::-1], jnp.int32),
            pltpu.VMEM(route_weights.shape[::-1], jnp.int32),
            pltpu.VMEM(residual.shape, bf16),
            pltpu.VMEM(norm_gain.shape, f32),
            pltpu.VMEM(kv_cache.shape, bf16),
            pltpu.VMEM(wo.shape, bf16),
            pltpu.VMEM(wgu.shape, bf16),
            pltpu.VMEM(wd.shape, bf16),
            pltpu.VMEM((rows, heads * groups, kv_width), f32),
            pltpu.VMEM((rows, heads * groups, kv_width), f32),
            pltpu.VMEM((rows * heads * groups, kv_width), f32),
            pltpu.VMEM((rows, width), bf16),
            pltpu.VMEM((rows, width), bf16),
            pltpu.VMEM((n, cap, width), bf16),
            pltpu.VMEM((n, cap, width), bf16),
            pltpu.VMEM((slots, width), f32),
            pltpu.VMEM((slots, width), bf16),
            pltpu.VMEM((2 * units, lanes), f32),
            pltpu.VMEM((-(-units // 128) * 128, lanes), f32),
            pltpu.VMEM((slots, half), bf16),
            pltpu.VMEM((slots, half), bf16),
            pltpu.VMEM((n, cap, half), bf16),
            pltpu.VMEM((n, cap, half), bf16),
            pltpu.VMEM((slots, half), f32),
            dma((12,)),
            dma((2,)),
            dma((n,)),
            dma((n,)),
            dma((n,)),
            dma((slots // 16,)),
            dma((slots // 16,)),
            dma((n,)),
            dma((n,)),
        ],
        compiler_params=pltpu.CompilerParams(
            collective_id=0, has_side_effects=True, vmem_limit_bytes=60 * 1024 * 1024
        ),
    )(
        positions,
        sink_logits,
        queries,
        new_kv,
        kv_cache,
        wo,
        route_ids.T,
        route_weights.T,
        residual,
        norm_gain,
        wgu,
        wd,
    )


def solution(mesh):
    in_specs = (
        P("grp", None),
        P("grp", "head", None),
        P("grp", "head", None, None),
        P("grp", "head", None),
        P("grp"),
        P("head", None),
        P("head", None, None),
        P(),
        P("grp", None),
        P("grp", None),
        P("grp", None, "head"),
        P("grp", "head", None),
    )
    out_specs = P("grp", "head")
    def body(*args):
        if fused_fits(mesh, args):
            return fused(mesh.shape["grp"], *args)
        return local(*args)

    return jax.shard_map(body, mesh=mesh, in_specs=in_specs, out_specs=out_specs, check_vma=False)
```
